128 devices in a mesh: round: 8 (over z, y_lo), strip: 16 (over y_hi, x, core).
Axes of the slice: x: 4, y: 4 (y_hi: 2, y_lo: 2; y = y_hi * 2 + y_lo), z: 4, core: 2. Of those that a mesh axis runs over, the one named last changes fastest.
Arguments:
- image: float32 [8, 2, 8192, 1024], P('round', None, 'strip'), may hold values from -6 to 6
- radii: int32 [2, 2], replicated, may hold values from 1 to 16, as said below
- plan: int32 [7, 8], replicated, may hold values from 0 to 7, as said below
Outputs:
- correlation: float32 [8, 7, 2, 1024, 128], P('round', None, None, 'strip')
The draws below stay inside these ranges and needn't reach their ends.
Inputs may be any that keep to these rules, and one draw needn't show every extreme that they name: radii[c, 0] is at most max(2, 4) and radii[c, 1] lies above 8; the outer radius of colour 0 is 16. Each row is a perfect matching of the 8 rounds: plan[m, r] != r and plan[m, plan[m, r]] = r; rows may repeat.
All inputs are finite; a program needn't handle non-finite values.
Results may differ from the reference program's by a relative error of at most 0.0003.
Values sent between devices are 32-bit elements; how exact they have to be, the bound alone decides.
No kernel may reach another device: no remote copies, remote signals or barrier semaphores. Data moves between devices by JAX's collectives and lax.ppermute only.
A program may use at most 128 MiB of HBM per device.

```python
import math
import jax
import jax.numpy as jnp
from jax import lax

COLOURS = 2
REACH = 16
DOWN = 8
MATCHES = 7
COLS = 1024
ROUNDS = 8
ROWS = 8192
STRIP_ROWS = 64
STRIP_COLS = 128
N_STRIP = 16


def draw_radii(key, part):
    key = jax.random.fold_in(key, 11)
    inner_key, outer_key = jax.random.split(key)
    inner = jax.random.randint(inner_key, (COLOURS,), 1, max(2, REACH // 4) + 1)
    outer = jax.random.randint(outer_key, (COLOURS,), REACH // 2 + 1, REACH + 1)
    outer = outer.at[0].set(REACH)
    return jnp.stack([inner, outer], axis=1).astype(jnp.int32)


def draw_plan(key, part):
    key = jax.random.fold_in(key, 29)
    final_round = ROUNDS - 1
    player = jnp.arange(ROUNDS, dtype=jnp.int32)
    circle = (final_round - player) % final_round
    base = jnp.where(player == final_round, 0, jnp.where(circle == player, final_round, circle)).astype(jnp.int32)
    row_keys = jax.random.split(key, MATCHES)

    def one_row(row_key):
        labels = jax.random.permutation(row_key, ROUNDS).astype(jnp.int32)
        inverse = jnp.argsort(labels, stable=True).astype(jnp.int32)
        return jnp.take(labels, jnp.take(base, inverse))
    return jax.vmap(one_row)(row_keys).astype(jnp.int32)


def shard_levels(own_key, dims, cuts, smallest, top_value):
    level = 1.0
    for position, shards_of in cuts:
        steps = jax.random.uniform(jax.random.fold_in(jax.random.fold_in(own_key, 6), position), (shards_of,), jnp.float32, smallest / len(cuts), top_value / len(cuts))
        level = level * jnp.repeat(jnp.exp(steps), dims[position] // shards_of).reshape((-1,) + (1,) * (len(dims) - 1 - position))
    return level


def gaussian(key, shape, spread, limit, cuts=(), held_as=jnp.bfloat16):
    array = jax.random.normal(key, shape, jnp.float32) * spread
    if len(cuts) > 0:
        array = shard_levels(key, shape, cuts, -0.22, 0.18) * array
    return jnp.clip(array, min=-limit, max=limit).astype(held_as)


def setup_inputs(seed: int = 0) -> dict:
    splits = jax.random.split(jax.random.key(seed), 4)
    return {
        "image": gaussian(splits[0], (ROUNDS, COLOURS, ROWS, COLS), 1.0, 6.0, ((0, 8), (2, 16)), jnp.float32),
        "radii": draw_radii(jax.random.fold_in(splits[3], 71), 0),
        "plan": draw_plan(jax.random.fold_in(splits[3], 71), 0),
    }


def kernel_weights(radii, filter_reach):
    offsets = jnp.arange(-filter_reach, filter_reach + 1).astype(jnp.int32)
    radius = radii.astype(jnp.int32)[..., None]
    sigma = radius.astype(jnp.float32) * 0.5
    offset_value = offsets.astype(jnp.float32)
    raw_weight = jnp.exp(-(offset_value * offset_value) / (2.0 * sigma * sigma))
    inside = jnp.abs(offsets) <= radius
    raw_weight = jnp.where(inside, raw_weight, jnp.zeros_like(raw_weight))
    return raw_weight / lax.optimization_barrier(jnp.sum(raw_weight, axis=-1, keepdims=True))

def reference(image, radii, plan):
    round_count, colour_count, row_total, col_total = image.shape
    weights = kernel_weights(radii, REACH)
    taps = weights.reshape(colour_count * 2, 1, 2 * REACH + 1)

    def filter_round(planes):
        vertical = lax.conv_general_dilated(planes[None], taps[:, :, :, None], (1, 1), ((REACH, REACH), (0, 0)), feature_group_count=colour_count, precision=lax.Precision.HIGHEST)
        both_maps = lax.conv_general_dilated(vertical, taps[:, :, None, :], (1, 1), ((0, 0), (REACH, REACH)), feature_group_count=2 * colour_count, precision=lax.Precision.HIGHEST)
        both_maps = both_maps.reshape(colour_count, 2, row_total, col_total)
        difference = both_maps[:, 0] - both_maps[:, 1]
        return difference.reshape(colour_count, row_total // DOWN, DOWN, col_total // DOWN, DOWN).mean(axis=(2, 4))
    coarse = lax.map(filter_round, image)
    blocks = coarse.reshape(round_count, colour_count, N_STRIP, STRIP_ROWS, STRIP_COLS)
    spectra = jnp.fft.fft2(blocks)
    tau_value = 0.002 * STRIP_ROWS * STRIP_COLS
    scale_back = math.sqrt(STRIP_ROWS * STRIP_COLS)

    def per_round(round_index):
        own_spec = spectra[round_index]

        def per_match(partner):
            other_spec = spectra[partner]
            cross = own_spec * jnp.conj(other_spec)
            cross_real = jnp.real(cross)
            cross_imag = jnp.imag(cross)
            modulus = jnp.sqrt(cross_real * cross_real + cross_imag * cross_imag + tau_value * tau_value)
            surface = jnp.real(jnp.fft.ifft2(cross / modulus)) * scale_back
            return surface.reshape(colour_count, N_STRIP * STRIP_ROWS, STRIP_COLS)
        return lax.map(per_match, plan[:, round_index].astype(jnp.int32))
    correlation = lax.map(per_round, jnp.arange(round_count).astype(jnp.int32))
    return correlation.astype(jnp.float32)
```

```python
import math

import jax
import jax.numpy as jnp
import ml_dtypes
import numpy as np
from jax import lax
from jax.experimental import pallas as pl
from jax.experimental.pallas import tpu as pltpu
from jax.sharding import PartitionSpec as P

REACH = 16
DOWN = 8
TAU_SCALE = 0.002
SPAN = 5
CHUNKS = 4
MIB = 1024 * 1024
VMEM = pl.BlockSpec(memory_space=pltpu.VMEM)
SMEM = pl.BlockSpec(memory_space=pltpu.SMEM)
HBM = pl.BlockSpec(memory_space=pltpu.HBM)


def halves(x):
    high = x.astype(jnp.bfloat16)
    return high, (x - high.astype(jnp.float32)).astype(jnp.bfloat16)


def dot(a, b):
    return jnp.dot(a, b, preferred_element_type=jnp.float32)


def np_halves(x):
    x = np.asarray(x, np.float32)
    high = x.astype(ml_dtypes.bfloat16)
    return high, (x - high.astype(np.float32)).astype(ml_dtypes.bfloat16)


def np_stacked(x):
    high, low = np_halves(x)
    return np.concatenate([high, high, low], axis=1)


def stacked_dot(table, x):
    high, low = halves(x)
    return dot(table[...], jnp.concatenate([high, low, high], axis=0))


def tables(rows, cols):
    half = rows // 2
    kept = half + 8
    u = np.arange(half + 1)[:, None] * np.arange(rows)[None, :] % rows
    v = np.arange(cols)[:, None] * np.arange(cols)[None, :] % cols
    row_cos, row_sin = np.cos(u * (2 * np.pi / rows)), np.sin(u * (2 * np.pi / rows))
    col_cos, col_sin = np.cos(v * (2 * np.pi / cols)), np.sin(v * (2 * np.pi / cols))
    fwd_row = np_stacked(np.concatenate([row_cos[:half], row_cos[half:], -row_sin[1:half]]))
    fwd_col = np_halves(np.block([[col_cos, -col_sin], [col_sin, col_cos]]))
    inv_col = np_halves(np.block([[col_cos, col_sin], [-col_sin, col_cos]]))
    scale = 1.0 / math.sqrt(rows * cols)
    back = np.zeros((2, kept, rows))
    back[0, 1:half] = 2.0 * scale * row_cos[1:half]
    back[1, 1:half] = -2.0 * scale * row_sin[1:half]
    back[0, half], back[0, half + 1] = scale * row_cos[0], scale * row_cos[half]
    inv_row = np_stacked(back.reshape(2 * kept, rows).T)
    return (fwd_row, *fwd_col), (fwd_col[0][:cols], fwd_col[1][:cols], *inv_col, inv_row)


def band_kernel(image, radii, col_high, col_low, taps, near, far, border, sems):
    colours, cols = col_high.shape[0], col_high.shape[1]
    rows = image.shape[2]
    copies = []
    for side, start in enumerate((0, rows - REACH)):
        copies.append(
            pltpu.make_async_copy(
                image.at[0, :, pl.ds(start, REACH)], border.at[:, pl.ds(side * REACH, REACH)], sems.at[side]
            )
        )
        copies[side].start()
    lane = lax.broadcasted_iota(jnp.int32, (8, 128), 1)
    row = lax.broadcasted_iota(jnp.int32, (8, 128), 0)
    offset = lane - 64
    t = offset.astype(jnp.float32)
    for c in range(colours):
        for j in range(2):
            radius = jnp.broadcast_to(radii[c : c + 1, j : j + 1], (8, 128))
            sigma = radius.astype(jnp.float32) * 0.5
            raw = jnp.where(jnp.abs(offset) <= radius, jnp.exp(-(t * t) / (2.0 * sigma * sigma)), 0.0)
            weight = raw / jnp.sum(raw, axis=1, keepdims=True)
            for e in range(SPAN):
                lag = row + 8 * (e - 2) - offset
                part = jnp.where((lag >= 0) & (lag < DOWN), weight, 0.0)
                total = jnp.sum(part, axis=1, keepdims=True) * (1.0 / DOWN)
                taps[c, j, e] = jnp.broadcast_to(total, (8, 128))

    for c in range(colours):
        for j in range(2):
            pair = []
            for step in range(2):
                block = jnp.zeros((8, 128), jnp.float32)
                for e in range(SPAN):
                    block = jnp.where(offset == step + 2 - e, taps[c, j, e], block)
                pair.append(block)
            tall = lax.broadcasted_iota(jnp.int32, (16, 128), 1)
            for half, out in zip(halves(jnp.concatenate(pair, axis=0)), (col_high, col_low)):
                half = half.astype(jnp.float32)
                for k in range(cols // 16):
                    turned = pltpu.roll(half, (2 * k - 64) % 128, 1)
                    if k == 0:
                        turned = jnp.where(tall < 64, turned, 0.0)
                    if k == cols // 16 - 1:
                        turned = jnp.where(tall >= 64, turned, 0.0)
                    out[c, 16 * k : 16 * k + 16, 128 * j : 128 * (j + 1)] = turned.astype(jnp.bfloat16)

    for copy in copies:
        copy.wait()
    odd = lax.rem(lax.axis_index("strip"), 2) == 1
    for c in range(colours):
        high, low = halves(border[c])
        across = dot(high, col_high[c]) + dot(low, col_high[c]) + dot(high, col_low[c])

        def reach(*terms):
            total = 0.0
            for block, e in terms:
                part = across[8 * block : 8 * block + 8]
                total = total + part[:, :128] * taps[c, 0, e + 2] - part[:, 128:] * taps[c, 1, e + 2]
            return jnp.broadcast_to(jnp.sum(total, axis=0, keepdims=True), (8, 128))

        up = jnp.where(row == 6, reach((0, 2)), jnp.where(row == 7, reach((0, 1), (1, 2)), 0.0))
        down = jnp.where(row == 0, reach((2, -2), (3, -1)), jnp.where(row == 1, reach((3, -2)), 0.0))
        near[c] = jnp.where(odd, up, down)
        far[c] = jnp.where(odd, down, up)


def across_kernel(image, col_high, col_low, across):
    _, colours, rows, _ = image.shape
    size = rows // CHUNKS
    for c in range(colours):
        for n in range(CHUNKS):
            at = slice(n * size, (n + 1) * size)
            high, low = halves(image[0, c, at])
            across[c, at] = dot(high, col_high[c]) + dot(low, col_high[c]) + dot(high, col_low[c])


def spectrum_kernel(across, taps, near, far, row_table, col_high, col_low, packed):
    colours, rows = across.shape[:2]
    blocks = rows // 8
    half, cols = packed.shape[2], packed.shape[3] // 2
    odd = lax.rem(lax.axis_index("strip"), 2) == 1
    edge = jnp.zeros((2, 8, 2 * cols), jnp.float32)
    gap = jnp.zeros((blocks - 16, cols), jnp.float32)
    coarse = []
    for c in range(colours):
        padded = jnp.concatenate([edge, across[c].reshape(blocks, 8, 2 * cols), edge], axis=0)
        total = 0.0
        for e in range(SPAN):
            part = padded[e : e + blocks]
            total = total + part[:, :, :cols] * taps[c, 0, e] - part[:, :, cols:] * taps[c, 1, e]
        above = jnp.where(odd, near[c], far[c])
        below = jnp.where(odd, far[c], near[c])
        coarse.append(jnp.sum(total, axis=1) + jnp.concatenate([above, gap, below], axis=0))
    first = stacked_dot(row_table, jnp.concatenate(coarse, axis=1))
    stacked = []
    for c in range(colours):
        lanes = slice(c * cols, (c + 1) * cols)
        stacked.append(jnp.concatenate([first[:half, lanes], first[half:, lanes]], axis=1))
    stacked = jnp.concatenate(stacked, axis=0)
    high, low = halves(stacked)
    whole = dot(high, col_high[...]) + dot(low, col_high[...]) + dot(high, col_low[...])
    row = lax.broadcasted_iota(jnp.int32, whole.shape, 0)
    whole = jnp.where(row % half == 0, stacked, whole).reshape(colours, half, 2 * cols)
    for k in range(packed.shape[0]):
        packed[k] = whole


def phase_kernel(tau, plan, packed, real_high, real_low, col_high, col_low, row_table, out, ends, surfaces, sems):
    me = lax.axis_index("round")
    matches, colours, rows, cols = out.shape[1:]
    rounds, half = packed.shape[0], packed.shape[2]
    kept = half + 8
    heads = packed[:, :, :8].reshape(rounds * colours * 8, 2 * cols)
    high, low = halves(heads)
    parts = []
    for lanes in (slice(0, cols), slice(cols, 2 * cols)):
        part = (
            dot(high[:, lanes], real_high[...])
            + dot(low[:, lanes], real_high[...])
            + dot(high[:, lanes], real_low[...])
        )
        parts.append(part.reshape(rounds, colours, 8, 2 * cols))
    row = lax.broadcasted_iota(jnp.int32, (1, 1, 8, 1), 2)
    last = jnp.concatenate([parts[1][:, :, 7:], parts[1][:, :, :7]], axis=2)
    ends[...] = jnp.where(row == 0, parts[0], jnp.where(row == 1, last, 0.0))
    table = row_table[...]

    def normalized(own, other):
        own_real, own_imag = own[:, :cols], own[:, cols:]
        other_real, other_imag = other[:, :cols], other[:, cols:]
        real = own_real * other_real + own_imag * other_imag
        imag = own_imag * other_real - own_real * other_imag
        scale = lax.rsqrt(real * real + imag * imag + tau * tau)
        return jnp.concatenate([real * scale, imag * scale], axis=1)

    stacked, copies = [], []
    for m in range(matches):
        partner = plan[m, me]
        for c in range(colours):
            stacked.append(normalized(packed[me, c], packed[partner, c]))
            stacked.append(normalized(ends[me, c], ends[partner, c]))
    high, low = halves(jnp.concatenate(stacked, axis=0))
    whole = dot(high, col_high[...]) + dot(low, col_high[...]) + dot(high, col_low[...])
    for m in range(matches):
        both = []
        for c in range(colours):
            at = (m * colours + c) * kept
            part = whole[at : at + kept]
            both.append(jnp.concatenate([part[:, :cols], part[:, cols:]], axis=0))
        surface = stacked_dot(table, jnp.concatenate(both, axis=1))
        for c in range(colours):
            surfaces[m, c] = surface[:, c * cols : (c + 1) * cols]
        copies.append(pltpu.make_async_copy(surfaces.at[m], out.at[0, m], sems.at[m]))
        copies[m].start()
    for copy in copies:
        copy.wait()


def per_device(image, radii, plan):
    _, colours, rows, cols = image.shape
    strip_rows, strip_cols = rows // DOWN, cols // DOWN
    strips, rounds = lax.axis_size("strip"), lax.axis_size("round")
    forward, backward = tables(strip_rows, strip_cols)
    forward, backward = [[jnp.asarray(table) for table in group] for group in (forward, backward)]

    f32, bf16 = jnp.float32, jnp.bfloat16
    border = jax.ShapeDtypeStruct((colours, 8, strip_cols), f32)
    col_high, col_low, taps, near, far = pl.pallas_call(
        band_kernel,
        out_shape=[
            jax.ShapeDtypeStruct((colours, cols, 2 * strip_cols), bf16),
            jax.ShapeDtypeStruct((colours, cols, 2 * strip_cols), bf16),
            jax.ShapeDtypeStruct((colours, 2, SPAN, 8, strip_cols), f32),
            border,
            border,
        ],
        in_specs=[HBM, VMEM],
        out_specs=[VMEM] * 5,
        scratch_shapes=[
            pltpu.VMEM((colours, 2 * REACH, cols), f32),
            pltpu.SemaphoreType.DMA((2,)),
        ],
        compiler_params=pltpu.CompilerParams(vmem_limit_bytes=8 * MIB),
        name="bands",
    )(pltpu.with_memory_space_constraint(image, pltpu.HBM), radii)
    near = lax.ppermute(near, "strip", [(i, i ^ 1) for i in range(strips)])
    far = lax.ppermute(
        far, "strip", [(i, i + 1 if i % 2 else i - 1) for i in range(1, strips - 1)]
    )
    across = pl.pallas_call(
        across_kernel,
        out_shape=jax.ShapeDtypeStruct((colours, rows, 2 * strip_cols), f32),
        in_specs=[VMEM] * 3,
        out_specs=VMEM,
        compiler_params=pltpu.CompilerParams(vmem_limit_bytes=24 * MIB),
        name="across",
    )(image, col_high, col_low)
    packed = pl.pallas_call(
        spectrum_kernel,
        out_shape=jax.ShapeDtypeStruct((rounds, colours, strip_rows // 2, 2 * strip_cols), f32),
        in_specs=[VMEM] * 7,
        out_specs=VMEM,
        compiler_params=pltpu.CompilerParams(vmem_limit_bytes=16 * MIB),
        name="spectrum",
    )(across, taps, near, far, *forward)
    packed = lax.all_to_all(packed, "round", 0, 0, tiled=True)
    tau = TAU_SCALE * strip_rows * strip_cols
    matches = plan.shape[0]
    return pl.pallas_call(
        lambda *refs: phase_kernel(tau, *refs),
        out_shape=jax.ShapeDtypeStruct((1, matches, colours, strip_rows, strip_cols), f32),
        in_specs=[SMEM] + [VMEM] * 6,
        out_specs=HBM,
        scratch_shapes=[
            pltpu.VMEM((rounds, colours, 8, 2 * strip_cols), f32),
            pltpu.VMEM((matches, colours, strip_rows, strip_cols), f32),
            pltpu.SemaphoreType.DMA((matches,)),
        ],
        compiler_params=pltpu.CompilerParams(vmem_limit_bytes=24 * MIB),
        name="phase",
    )(plan, packed, *backward)


def solution(mesh):
    in_specs = (P("round", None, "strip", None), P(), P())
    out_specs = P("round", None, None, "strip", None)
    return jax.shard_map(
        per_device, mesh=mesh, in_specs=in_specs, out_specs=out_specs, check_vma=False
    )
```

```python
import math

import jax
import jax.numpy as jnp
import ml_dtypes
import numpy as np
from jax import lax
from jax.experimental import pallas as pl
from jax.experimental.pallas import tpu as pltpu
from jax.sharding import PartitionSpec as P

REACH = 16
DOWN = 8
TAU_SCALE = 0.002
SPAN = 5
CHUNKS = 4
MIB = 1024 * 1024
VMEM = pl.BlockSpec(memory_space=pltpu.VMEM)
HBM = pl.BlockSpec(memory_space=pltpu.HBM)


def halves(x):
    high = x.astype(jnp.bfloat16)
    return high, (x - high.astype(jnp.float32)).astype(jnp.bfloat16)


def dot(a, b):
    return jnp.dot(a, b, preferred_element_type=jnp.float32)


def np_halves(x):
    x = np.asarray(x, np.float32)
    high = x.astype(ml_dtypes.bfloat16)
    return high, (x - high.astype(np.float32)).astype(ml_dtypes.bfloat16)


def np_stacked(x):
    high, low = np_halves(x)
    return np.concatenate([high, high, low], axis=1)


def stacked_dot(table, x):
    high, low = halves(x)
    return dot(table[...], jnp.concatenate([high, low, high], axis=0))


def tables(rows, cols):
    half = rows // 2
    kept = half + 8
    u = np.arange(half + 1)[:, None] * np.arange(rows)[None, :] % rows
    v = np.arange(cols)[:, None] * np.arange(cols)[None, :] % cols
    row_cos, row_sin = np.cos(u * (2 * np.pi / rows)), np.sin(u * (2 * np.pi / rows))
    col_cos, col_sin = np.cos(v * (2 * np.pi / cols)), np.sin(v * (2 * np.pi / cols))
    fwd_row = np.concatenate([row_cos[:half], row_cos[half:], -row_sin[1:half]])
    border = [np.repeat(fwd_row[:, h : h + 1], cols, axis=1) for h in (0, 1, rows - 2, rows - 1)]
    border = np.asarray(border, np.float32)
    fwd_row = np.concatenate(np_halves(np.repeat(fwd_row, DOWN, axis=1)))
    fwd_col = np_halves(np.block([[col_cos, -col_sin], [col_sin, col_cos]]))
    inv_col = np_halves(np.block([[col_cos, col_sin], [-col_sin, col_cos]]))
    scale = 1.0 / math.sqrt(rows * cols)
    back = np.zeros((2, kept, rows))
    back[0, 1:half] = 2.0 * scale * row_cos[1:half]
    back[1, 1:half] = -2.0 * scale * row_sin[1:half]
    back[0, half], back[0, half + 1] = scale * row_cos[0], scale * row_cos[half]
    inv_row = np_stacked(back.reshape(2 * kept, rows).T)
    return (fwd_row, border, *fwd_col), (fwd_col[0][:cols], fwd_col[1][:cols], *inv_col, inv_row)


def gathered(tiles, lane):
    total = 0.0
    for k, tile in enumerate(tiles):
        first = 2 if k == 0 else 0
        last = 34 if k == len(tiles) - 1 else 36
        folded = tile + pltpu.roll(tile, 64, 1)
        folded = jnp.where((lane >= first) & (lane < last), folded, 0.0)
        total = total + pltpu.roll(folded, (32 * k - 2) % 128, 1)
    return total


def grouped(x, table):
    rows, groups = x.shape[0], x.shape[1] // 256
    high, low = halves(jnp.concatenate([x[:, 256 * k : 256 * (k + 1)] for k in range(groups)], axis=0))
    both = dot(high, table) + dot(low, table)
    both = both[:, :128] + both[:, 128:]
    return [both[rows * k : rows * (k + 1)] for k in range(groups)]


def band_kernel(image, radii, table, taps, near, far, border, circle, sems):
    colours = table.shape[0]
    rows = image.shape[2]
    fetch = pltpu.make_async_copy(radii, circle, sems.at[2])
    fetch.start()
    copies = []
    for side, start in enumerate((0, rows - REACH)):
        copies.append(
            pltpu.make_async_copy(
                image.at[0, :, pl.ds(start, REACH)], border.at[:, pl.ds(side * REACH, REACH)], sems.at[side]
            )
        )
        copies[side].start()
    lane = lax.broadcasted_iota(jnp.int32, (8, 128), 1)
    row = lax.broadcasted_iota(jnp.int32, (8, 128), 0)
    offset = lane - 64
    t = offset.astype(jnp.float32)
    fetch.wait()
    for c in range(colours):
        columns = []
        for j in range(2):
            radius = jnp.broadcast_to(circle[c : c + 1, j : j + 1], (8, 128))
            sigma = radius.astype(jnp.float32) * 0.5
            raw = jnp.where(jnp.abs(offset) <= radius, jnp.exp(-(t * t) / (2.0 * sigma * sigma)), 0.0)
            weight = raw / jnp.sum(raw, axis=1, keepdims=True)
            for e in range(SPAN):
                lag = row + 8 * (e - 2) - offset
                part = jnp.where((lag >= 0) & (lag < DOWN), weight, 0.0)
                total = jnp.sum(part, axis=1, keepdims=True) * (1.0 / DOWN)
                columns.append(jnp.broadcast_to(total, (8, 128)))
        block = jnp.zeros((8, 128), jnp.float32)
        for e in range(SPAN):
            inner, outer = columns[e], columns[SPAN + e]
            taps[c, e] = jnp.where(lane < 64, inner, -outer)
            block = jnp.where(lane % 64 == SPAN - 1 - e, jnp.where(lane < 64, inner, outer), block)
        tall = jnp.concatenate([block, pltpu.roll(block, 1, 1)], axis=0)
        for side, half in enumerate(halves(tall)):
            half = half.astype(jnp.float32)
            for k in range(16):
                turned = pltpu.roll(half, 2 * k, 1) if k else half
                table[c, 16 * k : 16 * k + 16, 128 * side : 128 * (side + 1)] = turned.astype(jnp.bfloat16)

    for copy in copies:
        copy.wait()
    odd = lax.rem(lax.axis_index("strip"), 2) == 1
    for c in range(colours):
        ups, downs = [], []
        for part in grouped(border[c], table[c]):

            def reach(*terms):
                total = 0.0
                for block, e in terms:
                    total = total + part[8 * block : 8 * block + 8] * taps[c, e + 2]
                return jnp.broadcast_to(jnp.sum(total, axis=0, keepdims=True), (8, 128))

            ups.append(jnp.where(row == 6, reach((0, 2)), jnp.where(row == 7, reach((0, 1), (1, 2)), 0.0)))
            downs.append(jnp.where(row == 0, reach((2, -2), (3, -1)), jnp.where(row == 1, reach((3, -2)), 0.0)))
        up, down = gathered(ups, lane), gathered(downs, lane)
        near[c] = jnp.where(odd, up, down)
        far[c] = jnp.where(odd, down, up)


def rows_kernel(image, table, taps, row_halves, partial, across, row_table, sem):
    fetch = pltpu.make_async_copy(row_halves, row_table, sem)
    fetch.start()
    _, colours, rows, cols = image.shape
    size = rows // CHUNKS
    blocks = rows // 8
    half = row_table.shape[0] // 2
    groups = cols // 256
    lane = lax.broadcasted_iota(jnp.int32, (half, 128), 1)
    edge = jnp.zeros((2, 8, 128), jnp.float32)
    for c in range(colours):
        for n in range(CHUNKS):
            at = slice(n * size, (n + 1) * size)
            for k, part in enumerate(grouped(image[0, c, at], table[c])):
                across[k, at] = part
        tiles = []
        for k in range(groups):
            padded = jnp.concatenate([edge, across[k].reshape(blocks, 8, 128), edge], axis=0)
            total = 0.0
            for e in range(SPAN):
                total = total + padded[e : e + blocks] * taps[c, e]
            tiles.append(total.reshape(rows, 128))
        if c == 0:
            fetch.wait()
        for pair in range(groups // 2):
            high, low = halves(jnp.concatenate(tiles[2 * pair : 2 * pair + 2], axis=1))
            both = dot(row_table[...], high)
            both = both[:half] + both[half:] + dot(row_table[:half], low)
            tiles[2 * pair], tiles[2 * pair + 1] = both[:, :128], both[:, 128:]
        partial[:, 128 * c : 128 * (c + 1)] = gathered(tiles, lane)


def spectrum_kernel(partial, near, far, border_table, col_high, col_low, packed):
    colours = near.shape[0]
    half, cols = packed.shape[2], packed.shape[3] // 2
    odd = lax.rem(lax.axis_index("strip"), 2) == 1
    stacked = []
    for c in range(colours):
        lanes = slice(c * cols, (c + 1) * cols)
        above = jnp.where(odd, near[c], far[c])
        below = jnp.where(odd, far[c], near[c])
        first = partial[:, lanes]
        for k, line in enumerate((above[0:1], above[1:2], below[6:7], below[7:8])):
            first = first + border_table[k] * line
        stacked.append(jnp.concatenate([first[:half], first[half:]], axis=1))
    stacked = jnp.concatenate(stacked, axis=0)
    high, low = halves(stacked)
    whole = dot(high, col_high[...]) + dot(low, col_high[...]) + dot(high, col_low[...])
    row = lax.broadcasted_iota(jnp.int32, whole.shape, 0)
    whole = jnp.where(row % half == 0, stacked, whole).reshape(colours, half, 2 * cols)
    for k in range(packed.shape[0]):
        packed[k] = whole


def phase_kernel(tau, plan, packed, real_high, real_low, col_high, col_low, row_table, out, ends, surfaces, sems):
    me = lax.axis_index("round")
    matches, colours, rows, cols = out.shape[1:]
    rounds, half = packed.shape[0], packed.shape[2]
    kept = half + 8
    heads = packed[:, :, :8].reshape(rounds * colours * 8, 2 * cols)
    high, low = halves(heads)
    parts = []
    for lanes in (slice(0, cols), slice(cols, 2 * cols)):
        part = (
            dot(high[:, lanes], real_high[...])
            + dot(low[:, lanes], real_high[...])
            + dot(high[:, lanes], real_low[...])
        )
        parts.append(part.reshape(rounds, colours, 8, 2 * cols))
    row = lax.broadcasted_iota(jnp.int32, (1, 1, 8, 1), 2)
    last = jnp.concatenate([parts[1][:, :, 7:], parts[1][:, :, :7]], axis=2)
    ends[...] = jnp.where(row == 0, parts[0], jnp.where(row == 1, last, 0.0))
    table = row_table[...]

    def normalized(own, other):
        own_real, own_imag = own[:, :cols], own[:, cols:]
        other_real, other_imag = other[:, :cols], other[:, cols:]
        real = own_real * other_real + own_imag * other_imag
        imag = own_imag * other_real - own_real * other_imag
        scale = lax.rsqrt(real * real + imag * imag + tau * tau)
        return jnp.concatenate([real * scale, imag * scale], axis=1)

    chosen = lax.broadcasted_iota(jnp.int32, plan.shape, 1) == me
    chosen = jnp.where(chosen, plan[...].astype(jnp.float32), 0.0)
    partners = [jnp.sum(chosen[m : m + 1]).astype(jnp.int32) for m in range(matches)]
    stacked, copies = [], []
    for m in range(matches):
        partner = partners[m]
        for c in range(colours):
            stacked.append(normalized(packed[me, c], packed[partner, c]))
            stacked.append(normalized(ends[me, c], ends[partner, c]))
    high, low = halves(jnp.concatenate(stacked, axis=0))
    whole = dot(high, col_high[...]) + dot(low, col_high[...]) + dot(high, col_low[...])
    for m in range(matches):
        both = []
        for c in range(colours):
            at = (m * colours + c) * kept
            part = whole[at : at + kept]
            both.append(jnp.concatenate([part[:, :cols], part[:, cols:]], axis=0))
        surface = stacked_dot(table, jnp.concatenate(both, axis=1))
        for c in range(colours):
            surfaces[m, c] = surface[:, c * cols : (c + 1) * cols]
        copies.append(pltpu.make_async_copy(surfaces.at[m], out.at[0, m], sems.at[m]))
        copies[m].start()
    for copy in copies:
        copy.wait()


def per_device(image, radii, plan):
    _, colours, rows, cols = image.shape
    strip_rows, strip_cols = rows // DOWN, cols // DOWN
    strips, rounds = lax.axis_size("strip"), lax.axis_size("round")
    forward, backward = tables(strip_rows, strip_cols)
    forward, backward = [[jnp.asarray(table) for table in group] for group in (forward, backward)]

    f32, bf16 = jnp.float32, jnp.bfloat16
    border = jax.ShapeDtypeStruct((colours, 8, strip_cols), f32)
    table, taps, near, far = pl.pallas_call(
        band_kernel,
        out_shape=[
            jax.ShapeDtypeStruct((colours, 256, 256), bf16),
            jax.ShapeDtypeStruct((colours, SPAN, 8, 128), f32),
            border,
            border,
        ],
        in_specs=[HBM, HBM],
        out_specs=[VMEM] * 4,
        scratch_shapes=[
            pltpu.VMEM((colours, 2 * REACH, cols), f32),
            pltpu.VMEM(radii.shape, jnp.int32),
            pltpu.SemaphoreType.DMA((3,)),
        ],
        compiler_params=pltpu.CompilerParams(vmem_limit_bytes=8 * MIB),
        name="bands",
    )(
        pltpu.with_memory_space_constraint(image, pltpu.HBM),
        pltpu.with_memory_space_constraint(radii, pltpu.HBM),
    )
    image, near, far = lax.optimization_barrier((image, near, far))
    far = lax.ppermute(
        far, "strip", [(i, i + 1 if i % 2 else i - 1) for i in range(1, strips - 1)]
    )
    near = lax.ppermute(near, "strip", [(i, i ^ 1) for i in range(strips)])
    partial = pl.pallas_call(
        rows_kernel,
        out_shape=jax.ShapeDtypeStruct((strip_rows, colours * strip_cols), f32),
        in_specs=[VMEM] * 3 + [HBM],
        out_specs=VMEM,
        scratch_shapes=[
            pltpu.VMEM((cols // 256, rows, 128), f32),
            pltpu.VMEM(forward[0].shape, bf16),
            pltpu.SemaphoreType.DMA,
        ],
        compiler_params=pltpu.CompilerParams(vmem_limit_bytes=24 * MIB),
        name="rows",
    )(image, table, taps, pltpu.with_memory_space_constraint(forward[0], pltpu.HBM))
    packed = pl.pallas_call(
        spectrum_kernel,
        out_shape=jax.ShapeDtypeStruct((rounds, colours, strip_rows // 2, 2 * strip_cols), f32),
        in_specs=[VMEM] * 6,
        out_specs=VMEM,
        compiler_params=pltpu.CompilerParams(vmem_limit_bytes=16 * MIB),
        name="spectrum",
    )(partial, near, far, *forward[1:])
    packed = lax.all_to_all(packed, "round", 0, 0, tiled=True)
    tau = TAU_SCALE * strip_rows * strip_cols
    matches = plan.shape[0]
    return pl.pallas_call(
        lambda *refs: phase_kernel(tau, *refs),
        out_shape=jax.ShapeDtypeStruct((1, matches, colours, strip_rows, strip_cols), f32),
        in_specs=[VMEM] * 7,
        out_specs=HBM,
        scratch_shapes=[
            pltpu.VMEM((rounds, colours, 8, 2 * strip_cols), f32),
            pltpu.VMEM((matches, colours, strip_rows, strip_cols), f32),
            pltpu.SemaphoreType.DMA((matches,)),
        ],
        compiler_params=pltpu.CompilerParams(vmem_limit_bytes=24 * MIB),
        name="phase",
    )(plan, packed, *backward)


def solution(mesh):
    in_specs = (P("round", None, "strip", None), P(), P())
    out_specs = P("round", None, None, "strip", None)
    return jax.shard_map(
        per_device, mesh=mesh, in_specs=in_specs, out_specs=out_specs, check_vma=False
    )
```

```python
import math

import jax
import jax.numpy as jnp
import ml_dtypes
import numpy as np
from jax import lax
from jax.experimental import pallas as pl
from jax.experimental.pallas import tpu as pltpu
from jax.sharding import PartitionSpec as P

REACH = 16
DOWN = 8
TAU_SCALE = 0.002
SPAN = 5
CHUNKS = 8
MIB = 1024 * 1024
VMEM = pl.BlockSpec(memory_space=pltpu.VMEM)
HBM = pl.BlockSpec(memory_space=pltpu.HBM)


def halves(x):
    high = x.astype(jnp.bfloat16)
    return high, (x - high.astype(jnp.float32)).astype(jnp.bfloat16)


def dot(a, b):
    return jnp.dot(a, b, preferred_element_type=jnp.float32)


def np_halves(x):
    x = np.asarray(x, np.float32)
    high = x.astype(ml_dtypes.bfloat16)
    return high, (x - high.astype(np.float32)).astype(ml_dtypes.bfloat16)


def np_stacked(x):
    high, low = np_halves(x)
    return np.concatenate([high, high, low], axis=1)


def stacked_dot(table, x):
    high, low = halves(x)
    return dot(table[...], jnp.concatenate([high, low, high], axis=0))


def tables(rows, cols):
    half = rows // 2
    kept = half + 8
    u = np.arange(half + 1)[:, None] * np.arange(rows)[None, :] % rows
    v = np.arange(cols)[:, None] * np.arange(cols)[None, :] % cols
    row_cos, row_sin = np.cos(u * (2 * np.pi / rows)), np.sin(u * (2 * np.pi / rows))
    col_cos, col_sin = np.cos(v * (2 * np.pi / cols)), np.sin(v * (2 * np.pi / cols))
    fwd_row = np.concatenate([row_cos[:half], row_cos[half:], -row_sin[1:half]])
    border = [np.repeat(fwd_row[:, h : h + 1], cols, axis=1) for h in (0, 1, rows - 2, rows - 1)]
    border = np.asarray(border, np.float32)
    fwd_row = np.concatenate(np_halves(np.repeat(fwd_row, DOWN, axis=1)))
    fwd_col = np_halves(np.block([[col_cos, -col_sin], [col_sin, col_cos]]))
    inv_col = np_halves(np.block([[col_cos, col_sin], [-col_sin, col_cos]]))
    scale = 1.0 / math.sqrt(rows * cols)
    back = np.zeros((2, kept, rows))
    back[0, 1:half] = 2.0 * scale * row_cos[1:half]
    back[1, 1:half] = -2.0 * scale * row_sin[1:half]
    back[0, half], back[0, half + 1] = scale * row_cos[0], scale * row_cos[half]
    inv_row = np_stacked(back.reshape(2 * kept, rows).T)
    return (fwd_row, border, *fwd_col), (fwd_col[0][:cols], fwd_col[1][:cols], *inv_col, inv_row)


def gathered(tiles, lane):
    total = 0.0
    for k, tile in enumerate(tiles):
        first = 2 if k == 0 else 0
        last = 34 if k == len(tiles) - 1 else 36
        folded = tile + pltpu.roll(tile, 64, 1)
        folded = jnp.where((lane >= first) & (lane < last), folded, 0.0)
        total = total + pltpu.roll(folded, (32 * k - 2) % 128, 1)
    return total


def grouped(x, table):
    rows, groups = x.shape[0], x.shape[1] // 256
    high, low = halves(jnp.concatenate([x[:, 256 * k : 256 * (k + 1)] for k in range(groups)], axis=0))
    both = dot(high, table) + dot(low, table)
    both = both[:, :128] + both[:, 128:]
    return [both[rows * k : rows * (k + 1)] for k in range(groups)]


def band_kernel(image, radii, table, taps, near, far, border, circle, sems):
    colours = table.shape[0]
    rows = image.shape[2]
    fetch = pltpu.make_async_copy(radii, circle, sems.at[2])
    fetch.start()
    copies = []
    for side, start in enumerate((0, rows - REACH)):
        copies.append(
            pltpu.make_async_copy(
                image.at[0, :, pl.ds(start, REACH)], border.at[:, pl.ds(side * REACH, REACH)], sems.at[side]
            )
        )
        copies[side].start()
    lane = lax.broadcasted_iota(jnp.int32, (8, 128), 1)
    row = lax.broadcasted_iota(jnp.int32, (8, 128), 0)
    offset = lane - 64
    t = offset.astype(jnp.float32)
    fetch.wait()
    for c in range(colours):
        columns = []
        for j in range(2):
            radius = jnp.broadcast_to(circle[c : c + 1, j : j + 1], (8, 128))
            sigma = radius.astype(jnp.float32) * 0.5
            raw = jnp.where(jnp.abs(offset) <= radius, jnp.exp(-(t * t) / (2.0 * sigma * sigma)), 0.0)
            weight = raw / jnp.sum(raw, axis=1, keepdims=True)
            for e in range(SPAN):
                lag = row + 8 * (e - 2) - offset
                part = jnp.where((lag >= 0) & (lag < DOWN), weight, 0.0)
                total = jnp.sum(part, axis=1, keepdims=True) * (1.0 / DOWN)
                columns.append(jnp.broadcast_to(total, (8, 128)))
        block = jnp.zeros((8, 128), jnp.float32)
        for e in range(SPAN):
            inner, outer = columns[e], columns[SPAN + e]
            taps[c, e] = jnp.where(lane < 64, inner, -outer)
            block = jnp.where(lane % 64 == SPAN - 1 - e, jnp.where(lane < 64, inner, outer), block)
        tall = jnp.concatenate([block, pltpu.roll(block, 1, 1)], axis=0)
        for side, half in enumerate(halves(tall)):
            half = half.astype(jnp.float32)
            for k in range(16):
                turned = pltpu.roll(half, 2 * k, 1) if k else half
                table[c, 16 * k : 16 * k + 16, 128 * side : 128 * (side + 1)] = turned.astype(jnp.bfloat16)

    for copy in copies:
        copy.wait()
    odd = lax.rem(lax.axis_index("strip"), 2) == 1
    for c in range(colours):
        ups, downs = [], []
        for part in grouped(border[c], table[c]):

            def reach(*terms):
                total = 0.0
                for block, e in terms:
                    total = total + part[8 * block : 8 * block + 8] * taps[c, e + 2]
                return jnp.broadcast_to(jnp.sum(total, axis=0, keepdims=True), (8, 128))

            ups.append(jnp.where(row == 6, reach((0, 2)), jnp.where(row == 7, reach((0, 1), (1, 2)), 0.0)))
            downs.append(jnp.where(row == 0, reach((2, -2), (3, -1)), jnp.where(row == 1, reach((3, -2)), 0.0)))
        up, down = gathered(ups, lane), gathered(downs, lane)
        near[c] = jnp.where(odd, up, down)
        far[c] = jnp.where(odd, down, up)


def rows_kernel(image, table, taps, row_halves, partial, across, row_table, sem):
    fetch = pltpu.make_async_copy(row_halves, row_table, sem)
    fetch.start()
    _, colours, rows, cols = image.shape
    size = rows // CHUNKS
    blocks = rows // 8
    half = row_table.shape[0] // 2
    groups = cols // 256
    lane = lax.broadcasted_iota(jnp.int32, (half, 128), 1)
    edge = jnp.zeros((2, 8, 128), jnp.float32)
    for c in range(colours):
        for n in range(CHUNKS):
            at = slice(n * size, (n + 1) * size)
            for k, part in enumerate(grouped(image[0, c, at], table[c])):
                across[k, at] = part
        tiles = []
        for k in range(groups):
            padded = jnp.concatenate([edge, across[k].reshape(blocks, 8, 128), edge], axis=0)
            total = 0.0
            for e in range(SPAN):
                total = total + padded[e : e + blocks] * taps[c, e]
            tiles.append(total.reshape(rows, 128))
        if c == 0:
            fetch.wait()
        for pair in range(groups // 2):
            high, low = halves(jnp.concatenate(tiles[2 * pair : 2 * pair + 2], axis=1))
            both = dot(row_table[...], high)
            both = both[:half] + both[half:] + dot(row_table[:half], low)
            tiles[2 * pair], tiles[2 * pair + 1] = both[:, :128], both[:, 128:]
        partial[:, 128 * c : 128 * (c + 1)] = gathered(tiles, lane)


def spectrum_kernel(partial, near, far, border_table, col_high, col_low, packed):
    colours = near.shape[0]
    half, cols = packed.shape[2], packed.shape[3] // 2
    odd = lax.rem(lax.axis_index("strip"), 2) == 1
    stacked = []
    for c in range(colours):
        lanes = slice(c * cols, (c + 1) * cols)
        above = jnp.where(odd, near[c], far[c])
        below = jnp.where(odd, far[c], near[c])
        first = partial[:, lanes]
        for k, line in enumerate((above[0:1], above[1:2], below[6:7], below[7:8])):
            first = first + border_table[k] * line
        stacked.append(jnp.concatenate([first[:half], first[half:]], axis=1))
    stacked = jnp.concatenate(stacked, axis=0)
    high, low = halves(stacked)
    whole = dot(high, col_high[...]) + dot(low, col_high[...]) + dot(high, col_low[...])
    row = lax.broadcasted_iota(jnp.int32, whole.shape, 0)
    whole = jnp.where(row % half == 0, stacked, whole).reshape(colours, half, 2 * cols)
    for k in range(packed.shape[0]):
        packed[k] = whole


def phase_kernel(tau, plan, packed, real_high, real_low, col_high, col_low, row_table, out, ends, surfaces, sems):
    me = lax.axis_index("round")
    matches, colours, rows, cols = out.shape[1:]
    rounds, half = packed.shape[0], packed.shape[2]
    chosen = lax.broadcasted_iota(jnp.int32, plan.shape, 1) == me
    chosen = jnp.where(chosen, plan[...].astype(jnp.float32), 0.0)
    partners = [jnp.sum(chosen[m : m + 1]).astype(jnp.int32) for m in range(matches)]
    heads = packed[:, :, :8].reshape(rounds * colours * 8, 2 * cols)
    high, low = halves(heads)
    parts = []
    for lanes in (slice(0, cols), slice(cols, 2 * cols)):
        part = (
            dot(high[:, lanes], real_high[...])
            + dot(low[:, lanes], real_high[...])
            + dot(high[:, lanes], real_low[...])
        )
        parts.append(part.reshape(rounds, colours, 8, 2 * cols))
    row = lax.broadcasted_iota(jnp.int32, (1, 1, 8, 1), 2)
    last = jnp.concatenate([parts[1][:, :, 7:], parts[1][:, :, :7]], axis=2)
    ends[...] = jnp.where(row == 0, parts[0], jnp.where(row == 1, last, 0.0))
    table = row_table[...]

    def normalized(own, other):
        own_real, own_imag = own[:, :cols], own[:, cols:]
        other_real, other_imag = other[:, :cols], other[:, cols:]
        real = own_real * other_real + own_imag * other_imag
        imag = own_imag * other_real - own_real * other_imag
        scale = lax.rsqrt(real * real + imag * imag + tau * tau)
        return jnp.concatenate([real * scale, imag * scale], axis=1)

    places = [(m, c) for m in range(matches) for c in range(colours)]

    def columns(spectra, size):
        crossed = [normalized(spectra[me, c], spectra[partners[m], c]) for m, c in places]
        high, low = halves(jnp.concatenate(crossed, axis=0))
        whole = dot(high, col_high[...]) + dot(low, col_high[...]) + dot(high, col_low[...])
        return [whole[size * k : size * (k + 1)] for k in range(len(places))]

    inner, outer = columns(packed, half), columns(ends, 8)
    copies = []
    for m in range(matches):
        both = []
        for c in range(colours):
            part, last = inner[m * colours + c], outer[m * colours + c]
            both.append(
                jnp.concatenate([part[:, :cols], last[:, :cols], part[:, cols:], last[:, cols:]], axis=0)
            )
        surface = stacked_dot(table, jnp.concatenate(both, axis=1))
        for c in range(colours):
            surfaces[m, c] = surface[:, c * cols : (c + 1) * cols]
        copies.append(pltpu.make_async_copy(surfaces.at[m], out.at[0, m], sems.at[m]))
        copies[m].start()
    for copy in copies:
        copy.wait()


def per_device(image, radii, plan):
    _, colours, rows, cols = image.shape
    strip_rows, strip_cols = rows // DOWN, cols // DOWN
    strips, rounds = lax.axis_size("strip"), lax.axis_size("round")
    forward, backward = tables(strip_rows, strip_cols)
    forward, backward = [[jnp.asarray(table) for table in group] for group in (forward, backward)]

    f32, bf16 = jnp.float32, jnp.bfloat16
    border = jax.ShapeDtypeStruct((colours, 8, strip_cols), f32)
    table, taps, near, far = pl.pallas_call(
        band_kernel,
        out_shape=[
            jax.ShapeDtypeStruct((colours, 256, 256), bf16),
            jax.ShapeDtypeStruct((colours, SPAN, 8, 128), f32),
            border,
            border,
        ],
        in_specs=[HBM, HBM],
        out_specs=[VMEM] * 4,
        scratch_shapes=[
            pltpu.VMEM((colours, 2 * REACH, cols), f32),
            pltpu.VMEM(radii.shape, jnp.int32),
            pltpu.SemaphoreType.DMA((3,)),
        ],
        compiler_params=pltpu.CompilerParams(vmem_limit_bytes=8 * MIB),
        name="bands",
    )(
        pltpu.with_memory_space_constraint(image, pltpu.HBM),
        pltpu.with_memory_space_constraint(radii, pltpu.HBM),
    )
    image, near, far = lax.optimization_barrier((image, near, far))
    far = lax.ppermute(
        far, "strip", [(i, i + 1 if i % 2 else i - 1) for i in range(1, strips - 1)]
    )
    near = lax.ppermute(near, "strip", [(i, i ^ 1) for i in range(strips)])
    partial = pl.pallas_call(
        rows_kernel,
        out_shape=jax.ShapeDtypeStruct((strip_rows, colours * strip_cols), f32),
        in_specs=[VMEM] * 3 + [HBM],
        out_specs=VMEM,
        scratch_shapes=[
            pltpu.VMEM((cols // 256, rows, 128), f32),
            pltpu.VMEM(forward[0].shape, bf16),
            pltpu.SemaphoreType.DMA,
        ],
        compiler_params=pltpu.CompilerParams(vmem_limit_bytes=24 * MIB),
        name="rows",
    )(image, table, taps, pltpu.with_memory_space_constraint(forward[0], pltpu.HBM))
    packed = pl.pallas_call(
        spectrum_kernel,
        out_shape=jax.ShapeDtypeStruct((rounds, colours, strip_rows // 2, 2 * strip_cols), f32),
        in_specs=[VMEM] * 6,
        out_specs=VMEM,
        compiler_params=pltpu.CompilerParams(vmem_limit_bytes=16 * MIB),
        name="spectrum",
    )(partial, near, far, *forward[1:])
    packed = lax.all_to_all(packed, "round", 0, 0, tiled=True)
    tau = TAU_SCALE * strip_rows * strip_cols
    matches = plan.shape[0]
    return pl.pallas_call(
        lambda *refs: phase_kernel(tau, *refs),
        out_shape=jax.ShapeDtypeStruct((1, matches, colours, strip_rows, strip_cols), f32),
        in_specs=[VMEM] * 7,
        out_specs=HBM,
        scratch_shapes=[
            pltpu.VMEM((rounds, colours, 8, 2 * strip_cols), f32),
            pltpu.VMEM((matches, colours, strip_rows, strip_cols), f32),
            pltpu.SemaphoreType.DMA((matches,)),
        ],
        compiler_params=pltpu.CompilerParams(vmem_limit_bytes=24 * MIB),
        name="phase",
    )(plan, packed, *backward)


def solution(mesh):
    in_specs = (P("round", None, "strip", None), P(), P())
    out_specs = P("round", None, None, "strip", None)
    return jax.shard_map(
        per_device, mesh=mesh, in_specs=in_specs, out_specs=out_specs, check_vma=False
    )
```

```python
import math

import jax
import jax.numpy as jnp
import ml_dtypes
import numpy as np
from jax import lax
from jax.experimental import pallas as pl
from jax.experimental.pallas import tpu as pltpu
from jax.sharding import PartitionSpec as P

REACH = 16
DOWN = 8
TAU_SCALE = 0.002
SPAN = 5
CHUNKS = 8
MIB = 1024 * 1024
VMEM = pl.BlockSpec(memory_space=pltpu.VMEM)
HBM = pl.BlockSpec(memory_space=pltpu.HBM)


def halves(x):
    high = x.astype(jnp.bfloat16)
    return high, (x - high.astype(jnp.float32)).astype(jnp.bfloat16)


def dot(a, b):
    return jnp.dot(a, b, preferred_element_type=jnp.float32)


def np_halves(x):
    x = np.asarray(x, np.float32)
    high = x.astype(ml_dtypes.bfloat16)
    return high, (x - high.astype(np.float32)).astype(ml_dtypes.bfloat16)


def np_stacked(x):
    high, low = np_halves(x)
    return np.concatenate([high, high, low], axis=1)


def stacked_dot(table, x):
    high, low = halves(x)
    return dot(table[...], jnp.concatenate([high, low, high], axis=0))


def tables(rows, cols):
    half = rows // 2
    kept = half + 8
    u = np.arange(half + 1)[:, None] * np.arange(rows)[None, :] % rows
    v = np.arange(cols)[:, None] * np.arange(cols)[None, :] % cols
    row_cos, row_sin = np.cos(u * (2 * np.pi / rows)), np.sin(u * (2 * np.pi / rows))
    col_cos, col_sin = np.cos(v * (2 * np.pi / cols)), np.sin(v * (2 * np.pi / cols))
    fwd_row = np.concatenate([row_cos[:half], row_cos[half:], -row_sin[1:half]])
    border = [np.repeat(fwd_row[:, h : h + 1], cols, axis=1) for h in (0, 1, rows - 2, rows - 1)]
    border = np.asarray(border, np.float32)
    fwd_row = np.concatenate(np_halves(np.repeat(fwd_row, DOWN, axis=1)))
    fwd_col = np_halves(np.block([[col_cos, -col_sin], [col_sin, col_cos]]))
    inv_col = np_halves(np.block([[col_cos, col_sin], [-col_sin, col_cos]]))
    scale = 1.0 / math.sqrt(rows * cols)
    back = np.zeros((2, kept, rows))
    back[0, 1:half] = 2.0 * scale * row_cos[1:half]
    back[1, 1:half] = -2.0 * scale * row_sin[1:half]
    back[0, half], back[0, half + 1] = scale * row_cos[0], scale * row_cos[half]
    inv_row = np_stacked(back.reshape(2 * kept, rows).T)
    return (fwd_row, border, *fwd_col), (fwd_col[0][:cols], fwd_col[1][:cols], *inv_col, inv_row)


def gathered(tiles, lane):
    total = 0.0
    for k, tile in enumerate(tiles):
        first = 2 if k == 0 else 0
        last = 34 if k == len(tiles) - 1 else 36
        folded = tile + pltpu.roll(tile, 64, 1)
        folded = jnp.where((lane >= first) & (lane < last), folded, 0.0)
        total = total + pltpu.roll(folded, (32 * k - 2) % 128, 1)
    return total


def grouped(x, table):
    rows, groups = x.shape[0], x.shape[1] // 256
    high, low = halves(jnp.concatenate([x[:, 256 * k : 256 * (k + 1)] for k in range(groups)], axis=0))
    both = dot(high, table) + dot(low, table)
    both = both[:, :128] + both[:, 128:]
    return [both[rows * k : rows * (k + 1)] for k in range(groups)]


def band_kernel(image, radii, table, taps, near, far, border, circle, sems):
    colours = table.shape[0]
    rows = image.shape[2]
    fetch = pltpu.make_async_copy(radii, circle, sems.at[2])
    fetch.start()
    copies = []
    for side, start in enumerate((0, rows - REACH)):
        copies.append(
            pltpu.make_async_copy(
                image.at[0, :, pl.ds(start, REACH)], border.at[:, pl.ds(side * REACH, REACH)], sems.at[side]
            )
        )
        copies[side].start()
    lane = lax.broadcasted_iota(jnp.int32, (8, 128), 1)
    row = lax.broadcasted_iota(jnp.int32, (8, 128), 0)
    offset = lane - 64
    t = offset.astype(jnp.float32)
    fetch.wait()
    for c in range(colours):
        columns = []
        for j in range(2):
            radius = jnp.broadcast_to(circle[c : c + 1, j : j + 1], (8, 128))
            sigma = radius.astype(jnp.float32) * 0.5
            raw = jnp.where(jnp.abs(offset) <= radius, jnp.exp(-(t * t) / (2.0 * sigma * sigma)), 0.0)
            norm = DOWN * jnp.sum(raw, axis=1, keepdims=True)
            for e in range(SPAN):
                lag = row + 8 * (e - 2) - offset
                part = jnp.where((lag >= 0) & (lag < DOWN), raw, 0.0)
                total = jnp.sum(part, axis=1, keepdims=True) / norm
                columns.append(jnp.broadcast_to(total, (8, 128)))
        block = jnp.zeros((8, 128), jnp.float32)
        for e in range(SPAN):
            inner, outer = columns[e], columns[SPAN + e]
            taps[c, e] = jnp.where(lane < 64, inner, -outer)
            block = jnp.where(lane % 64 == SPAN - 1 - e, jnp.where(lane < 64, inner, outer), block)
        tall = jnp.concatenate([block, pltpu.roll(block, 1, 1)], axis=0)
        for side, half in enumerate(halves(tall)):
            half = half.astype(jnp.float32)
            for k in range(16):
                turned = pltpu.roll(half, 2 * k, 1) if k else half
                table[c, 16 * k : 16 * k + 16, 128 * side : 128 * (side + 1)] = turned.astype(jnp.bfloat16)

    for copy in copies:
        copy.wait()
    odd = lax.rem(lax.axis_index("strip"), 2) == 1
    for c in range(colours):
        ups, downs = [], []
        for part in grouped(border[c], table[c]):

            def reach(*terms):
                total = 0.0
                for block, e in terms:
                    total = total + part[8 * block : 8 * block + 8] * taps[c, e + 2]
                return jnp.broadcast_to(jnp.sum(total, axis=0, keepdims=True), (8, 128))

            ups.append(jnp.where(row == 6, reach((0, 2)), jnp.where(row == 7, reach((0, 1), (1, 2)), 0.0)))
            downs.append(jnp.where(row == 0, reach((2, -2), (3, -1)), jnp.where(row == 1, reach((3, -2)), 0.0)))
        up, down = gathered(ups, lane), gathered(downs, lane)
        near[c] = jnp.where(odd, up, down)
        far[c] = jnp.where(odd, down, up)


def rows_kernel(image, table, taps, row_halves, partial, across, row_table, sem):
    fetch = pltpu.make_async_copy(row_halves, row_table, sem)
    fetch.start()
    _, colours, rows, cols = image.shape
    size = rows // CHUNKS
    blocks = rows // 8
    half = row_table.shape[0] // 2
    groups = cols // 256
    lane = lax.broadcasted_iota(jnp.int32, (half, 128), 1)
    edge = jnp.zeros((2, 8, 128), jnp.float32)
    for c in range(colours):
        for n in range(CHUNKS):
            at = slice(n * size, (n + 1) * size)
            for k, part in enumerate(grouped(image[0, c, at], table[c])):
                across[k, at] = part
        tiles = []
        for k in range(groups):
            padded = jnp.concatenate([edge, across[k].reshape(blocks, 8, 128), edge], axis=0)
            total = 0.0
            for e in range(SPAN):
                total = total + padded[e : e + blocks] * taps[c, e]
            tiles.append(total.reshape(rows, 128))
        if c == 0:
            fetch.wait()
        for pair in range(groups // 2):
            high, low = halves(jnp.concatenate(tiles[2 * pair : 2 * pair + 2], axis=1))
            both = dot(row_table[...], high)
            both = both[:half] + both[half:] + dot(row_table[:half], low)
            tiles[2 * pair], tiles[2 * pair + 1] = both[:, :128], both[:, 128:]
        partial[:, 128 * c : 128 * (c + 1)] = gathered(tiles, lane)


def spectrum_kernel(partial, near, far, border_table, col_high, col_low, packed):
    colours = near.shape[0]
    half, cols = packed.shape[2], packed.shape[3] // 2
    odd = lax.rem(lax.axis_index("strip"), 2) == 1
    stacked = []
    for c in range(colours):
        lanes = slice(c * cols, (c + 1) * cols)
        above = jnp.where(odd, near[c], far[c])
        below = jnp.where(odd, far[c], near[c])
        first = partial[:, lanes]
        for k, line in enumerate((above[0:1], above[1:2], below[6:7], below[7:8])):
            first = first + border_table[k] * line
        stacked.append(jnp.concatenate([first[:half], first[half:]], axis=1))
    stacked = jnp.concatenate(stacked, axis=0)
    high, low = halves(stacked)
    whole = dot(high, col_high[...]) + dot(low, col_high[...]) + dot(high, col_low[...])
    row = lax.broadcasted_iota(jnp.int32, whole.shape, 0)
    whole = jnp.where(row % half == 0, stacked, whole).reshape(colours, half, 2 * cols)
    for k in range(packed.shape[0]):
        packed[k] = whole


def phase_kernel(tau, plan, packed, real_high, real_low, col_high, col_low, row_table, out, ends, surfaces, sems):
    me = lax.axis_index("round")
    matches, colours, rows, cols = out.shape[1:]
    rounds, half = packed.shape[0], packed.shape[2]
    chosen = lax.broadcasted_iota(jnp.int32, plan.shape, 1) == me
    chosen = jnp.where(chosen, plan[...].astype(jnp.float32), 0.0)
    partners = [jnp.sum(chosen[m : m + 1]).astype(jnp.int32) for m in range(matches)]
    heads = packed[:, :, :8].reshape(rounds * colours * 8, 2 * cols)
    high, low = halves(heads)
    parts = []
    for lanes in (slice(0, cols), slice(cols, 2 * cols)):
        part = (
            dot(high[:, lanes], real_high[...])
            + dot(low[:, lanes], real_high[...])
            + dot(high[:, lanes], real_low[...])
        )
        parts.append(part.reshape(rounds, colours, 8, 2 * cols))
    row = lax.broadcasted_iota(jnp.int32, (1, 1, 8, 1), 2)
    last = jnp.concatenate([parts[1][:, :, 7:], parts[1][:, :, :7]], axis=2)
    ends[...] = jnp.where(row == 0, parts[0], jnp.where(row == 1, last, 0.0))
    table = row_table[...]

    def normalized(own, other):
        own_real, own_imag = own[:, :cols], own[:, cols:]
        other_real, other_imag = other[:, :cols], other[:, cols:]
        real = own_real * other_real + own_imag * other_imag
        imag = own_imag * other_real - own_real * other_imag
        scale = lax.rsqrt(real * real + imag * imag + tau * tau)
        return jnp.concatenate([real * scale, imag * scale], axis=1)

    places = [(m, c) for m in range(matches) for c in range(colours)]

    def columns(spectra, size):
        crossed = [normalized(spectra[me, c], spectra[partners[m], c]) for m, c in places]
        high, low = halves(jnp.concatenate(crossed, axis=0))
        whole = dot(high, col_high[...]) + dot(low, col_high[...]) + dot(high, col_low[...])
        return [whole[size * k : size * (k + 1)] for k in range(len(places))]

    inner, outer = columns(packed, half), columns(ends, 8)
    copies = []
    for m in range(matches):
        both = []
        for c in range(colours):
            part, last = inner[m * colours + c], outer[m * colours + c]
            both.append(
                jnp.concatenate([part[:, :cols], last[:, :cols], part[:, cols:], last[:, cols:]], axis=0)
            )
        surface = stacked_dot(table, jnp.concatenate(both, axis=1))
        for c in range(colours):
            surfaces[m, c] = surface[:, c * cols : (c + 1) * cols]
        copies.append(pltpu.make_async_copy(surfaces.at[m], out.at[0, m], sems.at[m]))
        copies[m].start()
    for copy in copies:
        copy.wait()


def per_device(image, radii, plan):
    _, colours, rows, cols = image.shape
    strip_rows, strip_cols = rows // DOWN, cols // DOWN
    strips, rounds = lax.axis_size("strip"), lax.axis_size("round")
    forward, backward = tables(strip_rows, strip_cols)
    forward, backward = [[jnp.asarray(table) for table in group] for group in (forward, backward)]

    f32, bf16 = jnp.float32, jnp.bfloat16
    border = jax.ShapeDtypeStruct((colours, 8, strip_cols), f32)
    table, taps, near, far = pl.pallas_call(
        band_kernel,
        out_shape=[
            jax.ShapeDtypeStruct((colours, 256, 256), bf16),
            jax.ShapeDtypeStruct((colours, SPAN, 8, 128), f32),
            border,
            border,
        ],
        in_specs=[HBM, HBM],
        out_specs=[VMEM] * 4,
        scratch_shapes=[
            pltpu.VMEM((colours, 2 * REACH, cols), f32),
            pltpu.VMEM(radii.shape, jnp.int32),
            pltpu.SemaphoreType.DMA((3,)),
        ],
        compiler_params=pltpu.CompilerParams(vmem_limit_bytes=2 * MIB),
        name="bands",
    )(
        pltpu.with_memory_space_constraint(image, pltpu.HBM),
        pltpu.with_memory_space_constraint(radii, pltpu.HBM),
    )
    image, near, far = lax.optimization_barrier((image, near, far))
    far = lax.ppermute(
        far, "strip", [(i, i + 1 if i % 2 else i - 1) for i in range(1, strips - 1)]
    )
    near = lax.ppermute(near, "strip", [(i, i ^ 1) for i in range(strips)])
    partial = pl.pallas_call(
        rows_kernel,
        out_shape=jax.ShapeDtypeStruct((strip_rows, colours * strip_cols), f32),
        in_specs=[VMEM] * 3 + [HBM],
        out_specs=VMEM,
        scratch_shapes=[
            pltpu.VMEM((cols // 256, rows, 128), f32),
            pltpu.VMEM(forward[0].shape, bf16),
            pltpu.SemaphoreType.DMA,
        ],
        compiler_params=pltpu.CompilerParams(vmem_limit_bytes=24 * MIB),
        name="rows",
    )(image, table, taps, pltpu.with_memory_space_constraint(forward[0], pltpu.HBM))
    packed = pl.pallas_call(
        spectrum_kernel,
        out_shape=jax.ShapeDtypeStruct((rounds, colours, strip_rows // 2, 2 * strip_cols), f32),
        in_specs=[VMEM] * 6,
        out_specs=VMEM,
        compiler_params=pltpu.CompilerParams(vmem_limit_bytes=16 * MIB),
        name="spectrum",
    )(partial, near, far, *forward[1:])
    packed = lax.all_to_all(packed, "round", 0, 0, tiled=True)
    tau = TAU_SCALE * strip_rows * strip_cols
    matches = plan.shape[0]
    return pl.pallas_call(
        lambda *refs: phase_kernel(tau, *refs),
        out_shape=jax.ShapeDtypeStruct((1, matches, colours, strip_rows, strip_cols), f32),
        in_specs=[VMEM] * 7,
        out_specs=HBM,
        scratch_shapes=[
            pltpu.VMEM((rounds, colours, 8, 2 * strip_cols), f32),
            pltpu.VMEM((matches, colours, strip_rows, strip_cols), f32),
            pltpu.SemaphoreType.DMA((matches,)),
        ],
        compiler_params=pltpu.CompilerParams(vmem_limit_bytes=12 * MIB),
        name="phase",
    )(plan, packed, *backward)


def solution(mesh):
    in_specs = (P("round", None, "strip", None), P(), P())
    out_specs = P("round", None, None, "strip", None)
    return jax.shard_map(
        per_device, mesh=mesh, in_specs=in_specs, out_specs=out_specs, check_vma=False
    )
```

```python
import math

import jax
import jax.numpy as jnp
import ml_dtypes
import numpy as np
from jax import lax
from jax.experimental import pallas as pl
from jax.experimental.pallas import tpu as pltpu
from jax.sharding import PartitionSpec as P

REACH = 16
DOWN = 8
TAU_SCALE = 0.002
SPAN = 5
CHUNKS = 8
MIB = 1024 * 1024
VMEM = pl.BlockSpec(memory_space=pltpu.VMEM)
HBM = pl.BlockSpec(memory_space=pltpu.HBM)


def halves(x):
    high = x.astype(jnp.bfloat16)
    return high, (x - high.astype(jnp.float32)).astype(jnp.bfloat16)


def dot(a, b):
    return jnp.dot(a, b, preferred_element_type=jnp.float32)


def np_halves(x):
    x = np.asarray(x, np.float32)
    high = x.astype(ml_dtypes.bfloat16)
    return high, (x - high.astype(np.float32)).astype(ml_dtypes.bfloat16)


def np_stacked(x):
    high, low = np_halves(x)
    return np.concatenate([high, high, low], axis=1)


def stacked_dot(table, x):
    high, low = halves(x)
    return dot(table[...], jnp.concatenate([high, low, high], axis=0))


def tables(rows, cols):
    half = rows // 2
    kept = half + 8
    u = np.arange(half + 1)[:, None] * np.arange(rows)[None, :] % rows
    v = np.arange(cols)[:, None] * np.arange(cols)[None, :] % cols
    row_cos, row_sin = np.cos(u * (2 * np.pi / rows)), np.sin(u * (2 * np.pi / rows))
    col_cos, col_sin = np.cos(v * (2 * np.pi / cols)), np.sin(v * (2 * np.pi / cols))
    fwd_row = np.concatenate([row_cos[:half], row_cos[half:], -row_sin[1:half]])
    border = [np.repeat(fwd_row[:, h : h + 1], cols, axis=1) for h in (0, 1, rows - 2, rows - 1)]
    border = np.asarray(border, np.float32)
    fwd_row = np.concatenate(np_halves(np.repeat(fwd_row, DOWN, axis=1)))
    fwd_col = np_halves(np.block([[col_cos, -col_sin], [col_sin, col_cos]]))
    inv_col = np_halves(np.block([[col_cos, col_sin], [-col_sin, col_cos]]))
    scale = 1.0 / math.sqrt(rows * cols)
    back = np.zeros((2, kept, rows))
    back[0, 1:half] = 2.0 * scale * row_cos[1:half]
    back[1, 1:half] = -2.0 * scale * row_sin[1:half]
    back[0, half], back[0, half + 1] = scale * row_cos[0], scale * row_cos[half]
    inv_row = np_stacked(back.reshape(2 * kept, rows).T)
    return (fwd_row, border, *fwd_col), (fwd_col[0][:cols], fwd_col[1][:cols], *inv_col, inv_row)


def gathered(tiles, lane):
    total = 0.0
    for k, tile in enumerate(tiles):
        first = 2 if k == 0 else 0
        last = 34 if k == len(tiles) - 1 else 36
        folded = tile + pltpu.roll(tile, 64, 1)
        folded = jnp.where((lane >= first) & (lane < last), folded, 0.0)
        total = total + pltpu.roll(folded, (32 * k - 2) % 128, 1)
    return total


def grouped(x, table):
    rows, groups = x.shape[0], x.shape[1] // 256
    high, low = halves(jnp.concatenate([x[:, 256 * k : 256 * (k + 1)] for k in range(groups)], axis=0))
    both = dot(high, table) + dot(low, table)
    both = both[:, :128] + both[:, 128:]
    return [both[rows * k : rows * (k + 1)] for k in range(groups)]


def band_kernel(image, radii, table, taps, near, far, border, circle, sems):
    colours = table.shape[0]
    rows = image.shape[2]
    fetch = pltpu.make_async_copy(radii, circle, sems.at[2])
    fetch.start()
    copies = []
    for side, start in enumerate((0, rows - REACH)):
        copies.append(
            pltpu.make_async_copy(
                image.at[0, :, pl.ds(start, REACH)], border.at[:, pl.ds(side * REACH, REACH)], sems.at[side]
            )
        )
        copies[side].start()
    lane = lax.broadcasted_iota(jnp.int32, (8, 128), 1)
    row = lax.broadcasted_iota(jnp.int32, (8, 128), 0)
    offset = lane - 64
    t = offset.astype(jnp.float32)
    fetch.wait()
    for c in range(colours):
        columns = []
        for j in range(2):
            radius = jnp.broadcast_to(circle[c : c + 1, j : j + 1], (8, 128))
            sigma = radius.astype(jnp.float32) * 0.5
            raw = jnp.where(jnp.abs(offset) <= radius, jnp.exp(-(t * t) / (2.0 * sigma * sigma)), 0.0)
            norm = DOWN * jnp.sum(raw, axis=1, keepdims=True)
            for e in range(SPAN):
                lag = row + 8 * (e - 2) - offset
                part = jnp.where((lag >= 0) & (lag < DOWN), raw, 0.0)
                total = jnp.sum(part, axis=1, keepdims=True) / norm
                columns.append(jnp.broadcast_to(total, (8, 128)))
        block = jnp.zeros((8, 128), jnp.float32)
        for e in range(SPAN):
            inner, outer = columns[e], columns[SPAN + e]
            taps[c, e] = jnp.where(lane < 64, inner, -outer)
            block = jnp.where(lane % 64 == SPAN - 1 - e, jnp.where(lane < 64, inner, outer), block)
        tall = jnp.concatenate([block, pltpu.roll(block, 1, 1)], axis=0)
        for side, half in enumerate(halves(tall)):
            half = half.astype(jnp.float32)
            for k in range(16):
                turned = pltpu.roll(half, 2 * k, 1) if k else half
                table[c, 16 * k : 16 * k + 16, 128 * side : 128 * (side + 1)] = turned.astype(jnp.bfloat16)

    for copy in copies:
        copy.wait()
    odd = lax.rem(lax.axis_index("strip"), 2) == 1
    for c in range(colours):
        parts = grouped(border[c], table[c])

        def reach(*terms):
            tiles = [sum(part[8 * n : 8 * n + 8] * taps[c, e + 2] for n, e in terms) for part in parts]
            return jnp.broadcast_to(jnp.sum(gathered(tiles, lane), axis=0, keepdims=True), (8, 128))

        up = jnp.where(row == 6, reach((0, 2)), jnp.where(row == 7, reach((0, 1), (1, 2)), 0.0))
        down = jnp.where(row == 0, reach((2, -2), (3, -1)), jnp.where(row == 1, reach((3, -2)), 0.0))
        near[c] = jnp.where(odd, up, down)
        far[c] = jnp.where(odd, down, up)


def rows_kernel(image, table, taps, row_halves, partial, across, row_table, sem):
    fetch = pltpu.make_async_copy(row_halves, row_table, sem)
    fetch.start()
    _, colours, rows, cols = image.shape
    size = rows // CHUNKS
    blocks = rows // 8
    half = row_table.shape[0] // 2
    groups = cols // 256
    lane = lax.broadcasted_iota(jnp.int32, (half, 128), 1)
    edge = jnp.zeros((2, 8, 128), jnp.float32)
    for c in range(colours):
        for n in range(CHUNKS):
            at = slice(n * size, (n + 1) * size)
            for k, part in enumerate(grouped(image[0, c, at], table[c])):
                across[k, at] = part
        tiles = []
        for k in range(groups):
            padded = jnp.concatenate([edge, across[k].reshape(blocks, 8, 128), edge], axis=0)
            total = 0.0
            for e in range(SPAN):
                total = total + padded[e : e + blocks] * taps[c, e]
            tiles.append(total.reshape(rows, 128))
        if c == 0:
            fetch.wait()
        for pair in range(groups // 2):
            high, low = halves(jnp.concatenate(tiles[2 * pair : 2 * pair + 2], axis=1))
            both = dot(row_table[...], high)
            both = both[:half] + both[half:] + dot(row_table[:half], low)
            tiles[2 * pair], tiles[2 * pair + 1] = both[:, :128], both[:, 128:]
        partial[:, 128 * c : 128 * (c + 1)] = gathered(tiles, lane)


def spectrum_kernel(partial, near, far, border_table, col_high, col_low, packed):
    colours = near.shape[0]
    half, cols = packed.shape[2], packed.shape[3] // 2
    odd = lax.rem(lax.axis_index("strip"), 2) == 1
    stacked = []
    for c in range(colours):
        lanes = slice(c * cols, (c + 1) * cols)
        above = jnp.where(odd, near[c], far[c])
        below = jnp.where(odd, far[c], near[c])
        first = partial[:, lanes]
        for k, line in enumerate((above[0:1], above[1:2], below[6:7], below[7:8])):
            first = first + border_table[k] * line
        stacked.append(jnp.concatenate([first[:half], first[half:]], axis=1))
    stacked = jnp.concatenate(stacked, axis=0)
    high, low = halves(stacked)
    whole = dot(high, col_high[...]) + dot(low, col_high[...]) + dot(high, col_low[...])
    row = lax.broadcasted_iota(jnp.int32, whole.shape, 0)
    whole = jnp.where(row % half == 0, stacked, whole).reshape(colours, half, 2 * cols)
    for k in range(packed.shape[0]):
        packed[k] = whole


def phase_kernel(tau, plan, packed, real_high, real_low, col_high, col_low, row_table, out, ends, surfaces, sems):
    me = lax.axis_index("round")
    matches, colours, rows, cols = out.shape[1:]
    rounds, half = packed.shape[0], packed.shape[2]
    chosen = lax.broadcasted_iota(jnp.int32, plan.shape, 1) == me
    chosen = jnp.where(chosen, plan[...].astype(jnp.float32), 0.0)
    partners = [jnp.sum(chosen[m : m + 1]).astype(jnp.int32) for m in range(matches)]
    heads = packed[:, :, :8].reshape(rounds * colours * 8, 2 * cols)
    high, low = halves(heads)
    parts = []
    for lanes in (slice(0, cols), slice(cols, 2 * cols)):
        part = (
            dot(high[:, lanes], real_high[...])
            + dot(low[:, lanes], real_high[...])
            + dot(high[:, lanes], real_low[...])
        )
        parts.append(part.reshape(rounds, colours, 8, 2 * cols))
    row = lax.broadcasted_iota(jnp.int32, (1, 1, 8, 1), 2)
    last = jnp.concatenate([parts[1][:, :, 7:], parts[1][:, :, :7]], axis=2)
    ends[...] = jnp.where(row == 0, parts[0], jnp.where(row == 1, last, 0.0))
    table = row_table[...]

    def normalized(own, other):
        own_real, own_imag = own[:, :cols], own[:, cols:]
        other_real, other_imag = other[:, :cols], other[:, cols:]
        real = own_real * other_real + own_imag * other_imag
        imag = own_imag * other_real - own_real * other_imag
        scale = lax.rsqrt(real * real + imag * imag + tau * tau)
        return jnp.concatenate([real * scale, imag * scale], axis=1)

    places = [(m, c) for m in range(matches) for c in range(colours)]

    def columns(spectra, size):
        crossed = [normalized(spectra[me, c], spectra[partners[m], c]) for m, c in places]
        high, low = halves(jnp.concatenate(crossed, axis=0))
        whole = dot(high, col_high[...]) + dot(low, col_high[...]) + dot(high, col_low[...])
        return [whole[size * k : size * (k + 1)] for k in range(len(places))]

    inner, outer = columns(packed, half), columns(ends, 8)
    copies = []
    for m in range(matches):
        both = []
        for c in range(colours):
            part, last = inner[m * colours + c], outer[m * colours + c]
            both.append(
                jnp.concatenate([part[:, :cols], last[:, :cols], part[:, cols:], last[:, cols:]], axis=0)
            )
        surface = stacked_dot(table, jnp.concatenate(both, axis=1))
        for c in range(colours):
            surfaces[m, c] = surface[:, c * cols : (c + 1) * cols]
        copies.append(pltpu.make_async_copy(surfaces.at[m], out.at[0, m], sems.at[m]))
        copies[m].start()
    for copy in copies:
        copy.wait()


def per_device(image, radii, plan):
    _, colours, rows, cols = image.shape
    strip_rows, strip_cols = rows // DOWN, cols // DOWN
    strips, rounds = lax.axis_size("strip"), lax.axis_size("round")
    forward, backward = tables(strip_rows, strip_cols)
    forward, backward = [[jnp.asarray(table) for table in group] for group in (forward, backward)]

    f32, bf16 = jnp.float32, jnp.bfloat16
    border = jax.ShapeDtypeStruct((colours, 8, strip_cols), f32)
    table, taps, near, far = pl.pallas_call(
        band_kernel,
        out_shape=[
            jax.ShapeDtypeStruct((colours, 256, 256), bf16),
            jax.ShapeDtypeStruct((colours, SPAN, 8, 128), f32),
            border,
            border,
        ],
        in_specs=[HBM, HBM],
        out_specs=[VMEM] * 4,
        scratch_shapes=[
            pltpu.VMEM((colours, 2 * REACH, cols), f32),
            pltpu.VMEM(radii.shape, jnp.int32),
            pltpu.SemaphoreType.DMA((3,)),
        ],
        compiler_params=pltpu.CompilerParams(vmem_limit_bytes=2 * MIB),
        name="bands",
    )(
        pltpu.with_memory_space_constraint(image, pltpu.HBM),
        pltpu.with_memory_space_constraint(radii, pltpu.HBM),
    )
    image, near, far = lax.optimization_barrier((image, near, far))
    far = lax.ppermute(
        far, "strip", [(i, i + 1 if i % 2 else i - 1) for i in range(1, strips - 1)]
    )
    near = lax.ppermute(near, "strip", [(i, i ^ 1) for i in range(strips)])
    partial = pl.pallas_call(
        rows_kernel,
        out_shape=jax.ShapeDtypeStruct((strip_rows, colours * strip_cols), f32),
        in_specs=[VMEM] * 3 + [HBM],
        out_specs=VMEM,
        scratch_shapes=[
            pltpu.VMEM((cols // 256, rows, 128), f32),
            pltpu.VMEM(forward[0].shape, bf16),
            pltpu.SemaphoreType.DMA,
        ],
        compiler_params=pltpu.CompilerParams(vmem_limit_bytes=24 * MIB),
        name="rows",
    )(image, table, taps, pltpu.with_memory_space_constraint(forward[0], pltpu.HBM))
    packed = pl.pallas_call(
        spectrum_kernel,
        out_shape=jax.ShapeDtypeStruct((rounds, colours, strip_rows // 2, 2 * strip_cols), f32),
        in_specs=[VMEM] * 6,
        out_specs=VMEM,
        compiler_params=pltpu.CompilerParams(vmem_limit_bytes=16 * MIB),
        name="spectrum",
    )(partial, near, far, *forward[1:])
    packed = lax.all_to_all(packed, "round", 0, 0, tiled=True)
    tau = TAU_SCALE * strip_rows * strip_cols
    matches = plan.shape[0]
    return pl.pallas_call(
        lambda *refs: phase_kernel(tau, *refs),
        out_shape=jax.ShapeDtypeStruct((1, matches, colours, strip_rows, strip_cols), f32),
        in_specs=[VMEM] * 7,
        out_specs=HBM,
        scratch_shapes=[
            pltpu.VMEM((rounds, colours, 8, 2 * strip_cols), f32),
            pltpu.VMEM((matches, colours, strip_rows, strip_cols), f32),
            pltpu.SemaphoreType.DMA((matches,)),
        ],
        compiler_params=pltpu.CompilerParams(vmem_limit_bytes=12 * MIB),
        name="phase",
    )(plan, packed, *backward)


def solution(mesh):
    in_specs = (P("round", None, "strip", None), P(), P())
    out_specs = P("round", None, None, "strip", None)
    return jax.shard_map(
        per_device, mesh=mesh, in_specs=in_specs, out_specs=out_specs, check_vma=False
    )
```
